1024 devices in a mesh: dp: 8 (over y_lo, x), mp: 128 (over y_hi, z, core).
Axes of the slice: x: 4, y: 4 (y_hi: 2, y_lo: 2; y = y_hi * 2 + y_lo), z: 32, core: 2. Of those that a mesh axis runs over, the one named last changes fastest.
Arguments:
- tokens_in: bfloat16 [1024, 6144], P('dp', 'mp'), may hold values from -6 to 6
- in_weight: bfloat16 [6144, 24576], P(None, 'mp'), may hold values from -0.3125 to 0.3125
- hidden_grad: bfloat16 [1024, 24576], P('dp', 'mp'), may hold values from -4 to 4
Outputs:
- token_grad: bfloat16 [1024, 6144], P('dp', 'mp')
- weight_grad: float32 [6144, 24576], P('dp', 'mp')
The draws below stay inside these ranges and needn't reach their ends.
All inputs are finite; a program needn't handle non-finite values.
Results may differ from the reference program's by a relative error of at most 0.015.
Values may be sent and summed in bfloat16 or wider, within the bound.
A program may use at most 32 MiB of HBM per device.

```python
import jax
import jax.numpy as jnp
from jax import lax

D = 6144
FF = 24576
TOK_DEV = 128
TOKENS = 1024
N_DP = 8


def strengthened(entries, rng, source, target, shards_of, factor):
    owner, partner = [(jnp.arange(entries.shape[position]) // (entries.shape[position] // shards_of)).reshape([-1 if axis == position else 1 for axis in range(entries.ndim)]) for position in (source, target)]
    chosen = jax.random.permutation(rng, shards_of)[partner]
    strong = (owner == chosen) | (owner == (partner + shards_of // 2) % shards_of)
    return jnp.where(strong, factor * entries, entries)


def levels(stream_key, shape, shards, low, top_value):
    gain, own = 1.0, jax.random.fold_in(stream_key, 6)
    for axis_at, blocks in shards:
        draws = jnp.exp(jax.random.uniform(jax.random.fold_in(own, axis_at), (blocks,), jnp.float32, low / len(shards), top_value / len(shards)))
        gain = gain * jnp.repeat(draws, shape[axis_at] // blocks).reshape([-1 if axis == axis_at else 1 for axis in range(len(shape))])
    return gain


def noise(own_key, shape, spread, most, split=(), dtype=jnp.bfloat16):
    array = jax.random.normal(own_key, shape, jnp.float32) * spread
    if len(split) > 0:
        array = levels(own_key, shape, split, -0.22, 0.18) * array
    return jnp.clip(array, min=-most, max=most).astype(dtype)


def noise_with(own_key, dims, scale, reach, split, heavy, held_as=jnp.bfloat16):
    values = scale * jax.random.normal(own_key, dims, jnp.float32)
    if split:
        values = values * levels(own_key, dims, split, -0.22, 0.18)
    return jnp.clip(strengthened(values, jax.random.fold_in(own_key, 3), *heavy), -reach, reach).astype(held_as)


def setup_inputs(seed: int = 0) -> dict:
    key_of = jax.random.split(jax.random.key(seed), 4)
    tokens_in = noise(key_of[0], (TOKENS, D), 1.0, 6.0, ((0, 8), (1, 128)))
    in_weight = noise_with(key_of[1], (D, FF), D ** -0.5, 0.3125, ((1, 128),), (1, 0, 128, 5.5))
    hidden_grad = noise(key_of[2], (TOKENS, FF), 0.25, 4.0, ((0, 8), (1, 128)))
    return dict(tokens_in=tokens_in, in_weight=in_weight, hidden_grad=hidden_grad)


def gelu_slope(value):
    normal_cdf = 0.5 * (1.0 + lax.erf(value * 0.7071067811865476))
    density = jnp.exp(-0.5 * value * value) * 0.3989422804014327
    return normal_cdf + value * density


def reference(tokens_in, in_weight, hidden_grad):
    preact = jnp.dot(tokens_in, in_weight, preferred_element_type=jnp.float32)
    pre_grad = (hidden_grad.astype(jnp.float32) * gelu_slope(preact)).astype(jnp.bfloat16)
    token_grad = jnp.dot(pre_grad, in_weight.T, preferred_element_type=jnp.float32).astype(jnp.bfloat16)
    group_tokens = tokens_in.reshape(N_DP, TOK_DEV, D)
    group_grads = pre_grad.reshape(N_DP, TOK_DEV, FF)

    def add_group(total, pieces):
        partial_value = jnp.dot(pieces[0].T, pieces[1], preferred_element_type=jnp.float32)
        rounded = lax.optimization_barrier(partial_value.astype(jnp.bfloat16)).astype(jnp.float32)
        return total + rounded, None

    weight_grad, unused = lax.scan(add_group, jnp.zeros((D, FF), jnp.float32), (group_tokens, group_grads))
    return token_grad, weight_grad
```

```python
import jax
import jax.numpy as jnp
from jax import lax
from jax.experimental import pallas as pl
from jax.experimental.pallas import tpu as pltpu
from jax.sharding import PartitionSpec as P

MESH = pl.DeviceIdType.MESH
F32, BF16 = jnp.float32, jnp.bfloat16

NY, NG, NN, NC, NZ, NDP = 2, 8, 4, 2, 32, 8
CH, TOK, HID = 48, 128, 192
BLK = NN * NC * CH
NEAR = range(1, 8)


def gelu_slope(value):
    normal_cdf = 0.5 * (1.0 + lax.erf(value * 0.7071067811865476))
    density = jnp.exp(-0.5 * value * value) * 0.3989422804014327
    return normal_cdf + value * density


def ring(i):
    return ((i + 1) // 2) * (2 * (i % 2) - 1)


def kernel(
    x_ref, w_hbm, h_ref, tok_ref, wg_hbm,
    w, xt, acc, hgt, tp, sr, pair, near_in, far_out, far_in, xs, pga, wg,
    w_sem, wg_sem, own_sem,
    agf_s, agf_r, agn_s, agn_r, agc_s, agc_r,
    rsc_s, rsc_r, rsn_s, rsn_r, rsf_s, rsf_r,
    pg_s, pg_r, xs_s, xs_r, xc_s, xc_r,
):
    dp, mp = lax.axis_index("dp"), lax.axis_index("mp")
    yh, z, c = mp // 64, (mp // 2) % NZ, mp % 2
    g0, n = z // NN, z % NN
    sgn = 1 - 2 * c

    def at(dz, dy=0, core=c):
        return (dp, ((yh + dy) % NY) * 64 + ((z + dz + NZ) % NZ) * 2 + core)

    def send(src, dst, s, r, device):
        return pltpu.make_async_remote_copy(
            src_ref=src, dst_ref=dst, send_sem=s, recv_sem=r, device_id=device, device_id_type=MESH
        )

    def near_off(e):
        return e % 2, (0, 1, -1, 2 * sgn)[e // 2]

    def group(offset):
        return (g0 + offset + NG) % NG

    sibling = at(0, core=1 - c)
    far_z = (8, -8, 4, -4)

    load_w = pltpu.make_async_copy(w_hbm, w, w_sem)
    load_w.start()

    barrier = pltpu.get_barrier_semaphore()
    for dz in far_z:
        pl.semaphore_signal(barrier, inc=1, device_id=at(-dz), device_id_type=MESH)
    for e in NEAR:
        dy, dz = near_off(e)
        pl.semaphore_signal(barrier, inc=1, device_id=at(-dz, dy), device_id_type=MESH)
    pl.semaphore_signal(barrier, inc=1, device_id=sibling, device_id_type=MESH)
    for r in range(1, NDP):
        pl.semaphore_signal(barrier, inc=1, device_id=((dp - r + NDP) % NDP, mp), device_id_type=MESH)

    xt[yh, g0, n, c] = x_ref[...].astype(F32).T.astype(BF16)
    hgt[...] = h_ref[...].astype(F32).T
    acc[...] = jnp.zeros_like(acc)
    pl.semaphore_wait(barrier, 4 + 7 + 1 + 7)

    def ag_far(k):
        chunk = (0, 0, 0, 0, -2, 2, -2 * sgn)[k]
        dz = (8, -8, 4, -4, 4, -4, 8 * sgn)[k]
        ref = xt.at[yh, group(chunk), n, c]
        return send(ref, ref, agf_s.at[k], agf_r.at[k], at(dz))

    def ag_far_got(k):
        chunk = (-2, 2, -1, 1, -3, 3, 4)[k]
        ref = xt.at[yh, group(chunk), n, c]
        send(ref, ref, agf_s.at[k], agf_r.at[k], at(8)).wait_recv()

    def ag_near(g, e):
        dy, dz = near_off(e)
        ref = xt.at[yh, g, n, c]
        return send(ref, ref, agn_s.at[g, e - 1], agn_r.at[g, e - 1], at(dz, dy))

    def ag_near_start(i):
        g = group(ring(i))
        for e in NEAR:
            ag_near(g, e).start()

    def ag_near_got(g):
        for e in NEAR:
            dy, dz = near_off(e)
            ref = xt.at[(yh + dy) % NY, g, (z - dz + NZ) % NN, c]
            send(ref, ref, agn_s.at[g, e - 1], agn_r.at[g, e - 1], at(8)).wait_recv()

    def ag_core(g, core):
        ref = xt.at[:, g, :, core]
        return send(ref, ref, agc_s.at[g], agc_r.at[g], sibling)

    def rows_of(y, g):
        return pl.ds(pl.multiple_of((y * NG + g) * BLK, BLK), BLK)

    def pass_on(i):
        g = group(ring(i))
        ag_near_got(g)
        ag_core(g, c).start()

    def multiply(i):
        g = group(ring(i))
        ag_core(g, 1 - c).wait_recv()
        total = acc[...]
        for y in range(NY):
            total += lax.dot_general(
                w[rows_of(y, g), :], xt[y, g].reshape(BLK, TOK),
                (((0,), (0,)), ((), ())), preferred_element_type=F32,
            )
        acc[...] = total

    def loop(low, high, *steps):
        def body(i, carry):
            for step in steps:
                step(i)
            return carry

        lax.fori_loop(low, high, body, 0)

    for k in range(4):
        ag_far(k).start()
    ag_near_start(0)
    ag_far_got(0)
    ag_far_got(1)
    for k in (6, 4, 5):
        ag_far(k).start()
    ag_far_got(2)
    ag_far_got(3)
    loop(1, 5, ag_near_start)
    load_w.wait()
    pass_on(0)
    ag_far_got(4)
    ag_far_got(5)
    loop(5, 7, ag_near_start)
    ag_far_got(6)
    ag_near_start(7)
    pass_on(1)
    loop(2, 8, pass_on, lambda i: multiply(i - 2))
    multiply(6)
    multiply(7)

    pga[dp] = (hgt[...] * gelu_slope(acc[...])).astype(BF16)
    pgt = pga[dp]

    def rs_core(g):
        return send(tp.at[:, g, :, 1 - c], sr.at[:, g], rsc_s.at[g], rsc_r.at[g], sibling)

    def partial(i):
        g = group(ring(i))
        for y in range(NY):
            part = jnp.dot(w[rows_of(y, g), :], pgt, preferred_element_type=F32)
            tp[y, g] = part.astype(BF16).reshape(NN, NC, CH, TOK)
        rs_core(g).start()

    def rs_near(g, e):
        dy, dz = near_off(e)
        src = pair.at[(yh + dy) % NY, g, (z + dz + NZ) % NN]
        return send(src, near_in.at[g, e - 1], rsn_s.at[g, e - 1], rsn_r.at[g, e - 1], at(dz, dy))

    def pair_up(i):
        g = group(ring(i))
        rs_core(g).wait_recv()
        for y in range(NY):
            pair[y, g] = (tp[y, g, :, c].astype(F32) + sr[y, g].astype(F32)).astype(BF16)
        for e in NEAR:
            rs_near(g, e).start()

    def near_sum(offset):
        g = group(offset)
        total = pair[yh, g, n].astype(F32)
        for e in NEAR:
            rs_near(g, e).wait_recv()
        for e in NEAR:
            total += near_in[g, e - 1].astype(F32)
        return total

    def rs_far(k):
        dz = (8, -8, 8 * sgn, 4, -4, 8 * sgn, -8 * sgn)[k]
        return send(far_out.at[k], far_in.at[k], rsf_s.at[k], rsf_r.at[k], at(dz))

    def rs_far_start(k, value):
        far_out[k] = value.astype(BF16)
        rs_far(k).start()

    def rs_far_got(k):
        rs_far(k).wait_recv()
        return far_in[k].astype(F32)

    def slice_of(p, half):
        return p // 4, 2 * (p % 4) + half

    def pg_send(r):
        return send(pga.at[dp], pga.at[dp], pg_s.at[r - 1], pg_r.at[r - 1], ((dp + r) % NDP, mp))

    def pg_got(r):
        ref = pga.at[(dp - r + NDP) % NDP]
        send(ref, ref, pg_s.at[r - 1], pg_r.at[r - 1], sibling).wait_recv()

    def xs_send(r):
        to = (dp + r) % NDP
        y, g = slice_of(to, c)
        return send(xt.at[y, g], xs.at[dp, c], xs_s.at[r - 1], xs_r.at[r - 1], (to, mp))

    def xs_got(r):
        ref = xs.at[(dp - r + NDP) % NDP, c]
        send(ref, ref, xs_s.at[r - 1], xs_r.at[r - 1], sibling).wait_recv()

    def xc_copy(r, half):
        ref = xs.at[(dp - r + NDP) % NDP, half]
        return send(ref, ref, xc_s.at[r - 1], xc_r.at[r - 1], sibling)

    loop(5, 8, partial)
    loop(3, 5, partial)
    loop(5, 8, pair_up)
    loop(1, 3, partial)
    loop(3, 5, pair_up)
    partial(0)
    loop(1, 3, pair_up)
    pair_up(0)
    own_copies = []
    for half in range(2):
        y, g = slice_of(dp, half)
        own_copies.append(pltpu.make_async_copy(xt.at[y, g], xs.at[dp, half], own_sem.at[half]))
        own_copies[-1].start()
    for r in range(1, NDP):
        pg_send(r).start()
    for r in range(1, NDP):
        xs_send(r).start()

    for k in range(7):
        ag_far(k).wait_send()

    def ag_sent(g):
        for e in NEAR:
            ag_near(g, e).wait_send()
        ag_core(g, c).wait_send()

    loop(0, NG, ag_sent)

    rs_far_start(0, near_sum(3))
    rs_far_start(1, near_sum(-3))
    rs_far_start(2, near_sum(4))
    rs_far_start(6, near_sum(-2 * sgn))
    ahead = near_sum(2 * sgn)
    right, left = near_sum(1), near_sum(-1)
    mine = near_sum(0)
    for r in range(1, NDP):
        xs_got(r)
        xc_copy(r, c).start()
    rs_far_start(3, right + rs_far_got(0))
    rs_far_start(4, left + rs_far_got(1))
    rs_far_start(5, ahead + rs_far_got(2))

    for copy in own_copies:
        copy.wait()
    for r in range(1, NDP):
        pg_got(r)
        xc_copy(r, 1 - c).wait_recv()

    def weight_rows(i):
        half, quarter = i // 2, i % 2
        total = jnp.zeros((BLK // 2, HID), F32)
        for p in range(NDP):
            total += lax.dot_general(
                xs[p, half, pl.ds(2 * quarter, 2)].reshape(BLK // 2, TOK), pga[p],
                (((1,), (1,)), ((), ())), preferred_element_type=F32,
            )
        wg[pl.ds(pl.multiple_of(i * (BLK // 2), BLK // 2), BLK // 2), :] = total

    loop(0, 4, weight_rows)
    store_wg = pltpu.make_async_copy(wg, wg_hbm, wg_sem)
    store_wg.start()

    def rs_sent(g):
        for e in NEAR:
            rs_near(g, e).wait_send()
        rs_core(g).wait_send()

    loop(0, NG, rs_sent)
    for r in range(1, NDP):
        pg_send(r).wait_send()
        xs_send(r).wait_send()
        xc_copy(r, c).wait_send()

    for k in (3, 4, 5, 6):
        mine += rs_far_got(k)
    tok_ref[...] = mine.T.astype(BF16)
    for k in range(7):
        rs_far(k).wait_send()
    store_wg.wait()


def local(tokens_in, in_weight, hidden_grad):
    vmem, dma = pltpu.VMEM, pltpu.SemaphoreType.DMA
    features = in_weight.shape[0]
    return pl.pallas_call(
        kernel,
        out_shape=(
            jax.ShapeDtypeStruct((TOK, CH), BF16),
            jax.ShapeDtypeStruct((features // NDP, HID), F32),
        ),
        in_specs=[
            pl.BlockSpec(memory_space=pltpu.VMEM),
            pl.BlockSpec(memory_space=pl.ANY),
            pl.BlockSpec(memory_space=pltpu.VMEM),
        ],
        out_specs=(pl.BlockSpec(memory_space=pltpu.VMEM), pl.BlockSpec(memory_space=pl.ANY)),
        scratch_shapes=[
            vmem((features, HID), BF16),
            vmem((NY, NG, NN, NC, CH, TOK), BF16),
            vmem((HID, TOK), F32),
            vmem((HID, TOK), F32),
            vmem((NY, NG, NN, NC, CH, TOK), BF16),
            vmem((NY, NG, NN, CH, TOK), BF16),
            vmem((NY, NG, NN, CH, TOK), BF16),
            vmem((NG, 7, CH, TOK), BF16),
            vmem((7, CH, TOK), BF16),
            vmem((7, CH, TOK), BF16),
            vmem((NDP, 2, NN, NC, CH, TOK), BF16),
            vmem((NDP, HID, TOK), BF16),
            vmem((features // NDP, HID), F32),
            dma, dma, dma((2,)),
            dma((7,)), dma((7,)), dma((NG, 7)), dma((NG, 7)), dma((NG,)), dma((NG,)),
            dma((NG,)), dma((NG,)), dma((NG, 7)), dma((NG, 7)), dma((7,)), dma((7,)),
            dma((7,)), dma((7,)), dma((7,)), dma((7,)), dma((7,)), dma((7,)),
        ],
        compiler_params=pltpu.CompilerParams(
            collective_id=0, has_side_effects=True, vmem_limit_bytes=40 * 2**20
        ),
        cost_estimate=pl.CostEstimate(
            flops=6 * TOK * features * HID, bytes_accessed=4 * 2**20, transcendentals=2 * TOK * HID
        ),
    )(tokens_in, in_weight, hidden_grad)


def solution(mesh):
    in_specs = (P("dp", "mp"), P(None, "mp"), P("dp", "mp"))
    out_specs = (P("dp", "mp"), P("dp", "mp"))
    return jax.shard_map(local, mesh=mesh, in_specs=in_specs, out_specs=out_specs, check_vma=False)
```

```python
import jax
import jax.numpy as jnp
from jax import lax
from jax.experimental import pallas as pl
from jax.experimental.pallas import tpu as pltpu
from jax.sharding import PartitionSpec as P

MESH = pl.DeviceIdType.MESH
F32, BF16 = jnp.float32, jnp.bfloat16

NY, NG, NN, NC, NZ, NDP = 2, 8, 4, 2, 32, 8
CH, TOK, HID = 48, 128, 192
BLK = NN * NC * CH
NEAR = range(1, 8)


def gelu_slope(value):
    normal_cdf = 0.5 * (1.0 + lax.erf(value * 0.7071067811865476))
    density = jnp.exp(-0.5 * value * value) * 0.3989422804014327
    return normal_cdf + value * density


def ring(i):
    return ((i + 1) // 2) * (2 * (i % 2) - 1)


def kernel(
    x_hbm, w_hbm, h_hbm, tok_hbm, wg_hbm,
    w, wt, hg, tok, xt, acc, tp, sr, pair, near_in, far_out, far_in, xs, pga, wg,
    in_sem, out_sem, own_sem,
    agf_s, agf_r, agn_s, agn_r, agc_s, agc_r,
    rsc_s, rsc_r, rsn_s, rsn_r, rsf_s, rsf_r,
    pg_s, pg_r, xs_s, xs_r, xc_s, xc_r,
):
    dp, mp = lax.axis_index("dp"), lax.axis_index("mp")
    yh, z, c = mp // 64, (mp // 2) % NZ, mp % 2
    g0, n = z // NN, z % NN
    sgn = 1 - 2 * c

    def at(dz, dy=0, core=c):
        return (dp, ((yh + dy) % NY) * 64 + ((z + dz + NZ) % NZ) * 2 + core)

    def send(src, dst, s, r, device):
        return pltpu.make_async_remote_copy(
            src_ref=src, dst_ref=dst, send_sem=s, recv_sem=r, device_id=device, device_id_type=MESH
        )

    def near_off(e):
        return e % 2, (0, 1, -1, 2 * sgn)[e // 2]

    def group(offset):
        return (g0 + offset + NG) % NG

    sibling = at(0, core=1 - c)
    far_z = (8, -8, 4, -4)

    load_x = pltpu.make_async_copy(x_hbm, xt.at[yh, g0, n, c], in_sem.at[0])
    load_w = pltpu.make_async_copy(w_hbm, w, in_sem.at[1])
    load_h = pltpu.make_async_copy(h_hbm, hg, in_sem.at[2])

    barrier = pltpu.get_barrier_semaphore()
    for dz in far_z:
        pl.semaphore_signal(barrier, inc=1, device_id=at(-dz), device_id_type=MESH)
    for e in NEAR:
        dy, dz = near_off(e)
        pl.semaphore_signal(barrier, inc=1, device_id=at(-dz, dy), device_id_type=MESH)
    pl.semaphore_signal(barrier, inc=1, device_id=sibling, device_id_type=MESH)
    for r in range(1, NDP):
        pl.semaphore_signal(barrier, inc=1, device_id=((dp - r + NDP) % NDP, mp), device_id_type=MESH)

    load_x.start()
    load_w.start()
    load_h.start()
    acc[...] = jnp.zeros_like(acc)
    load_x.wait()
    pl.semaphore_wait(barrier, 4 + 7 + 1 + 7)

    def ag_far(k):
        chunk = (0, 0, 0, 0, -2, 2, -2 * sgn)[k]
        dz = (8, -8, 4, -4, 4, -4, 8 * sgn)[k]
        ref = xt.at[yh, group(chunk), n, c]
        return send(ref, ref, agf_s.at[k], agf_r.at[k], at(dz))

    def ag_far_got(k):
        chunk = (-2, 2, -1, 1, -3, 3, 4)[k]
        ref = xt.at[yh, group(chunk), n, c]
        send(ref, ref, agf_s.at[k], agf_r.at[k], at(8)).wait_recv()

    def ag_near(g, e):
        dy, dz = near_off(e)
        ref = xt.at[yh, g, n, c]
        return send(ref, ref, agn_s.at[g, e - 1], agn_r.at[g, e - 1], at(dz, dy))

    def ag_near_start(i):
        g = group(ring(i))
        for e in NEAR:
            ag_near(g, e).start()

    def ag_near_got(g):
        for e in NEAR:
            dy, dz = near_off(e)
            ref = xt.at[(yh + dy) % NY, g, (z - dz + NZ) % NN, c]
            send(ref, ref, agn_s.at[g, e - 1], agn_r.at[g, e - 1], at(8)).wait_recv()

    def ag_core(g, core):
        ref = xt.at[:, g, :, core]
        return send(ref, ref, agc_s.at[g], agc_r.at[g], sibling)

    def weights_of(y, g):
        return w[:, pl.ds(pl.multiple_of((y * NG + g) * BLK, BLK), BLK)]

    def pass_on(i):
        g = group(ring(i))
        ag_near_got(g)
        ag_core(g, c).start()

    def multiply(i):
        g = group(ring(i))
        ag_core(g, 1 - c).wait_recv()
        total = acc[...]
        for y in range(NY):
            total += jnp.dot(
                weights_of(y, g), xt[y, g].reshape(BLK, TOK), preferred_element_type=F32
            )
        acc[...] = total

    def turn(b):
        at_b = pl.ds(pl.multiple_of(b * BLK, BLK), BLK)
        wt[at_b, :] = w[:, at_b].T

    def loop(low, high, *steps):
        def body(i, carry):
            for step in steps:
                step(i)
            return carry

        lax.fori_loop(low, high, body, 0)

    for k in range(4):
        ag_far(k).start()
    ag_near_start(0)
    load_w.wait()
    load_h.wait()
    loop(0, NY * NG, turn)
    ag_far_got(0)
    ag_far_got(1)
    for k in (6, 4, 5):
        ag_far(k).start()
    ag_far_got(2)
    ag_far_got(3)
    loop(1, 5, ag_near_start)
    pass_on(0)
    ag_far_got(4)
    ag_far_got(5)
    loop(5, 7, ag_near_start)
    ag_far_got(6)
    ag_near_start(7)
    pass_on(1)
    loop(2, 8, pass_on, lambda i: multiply(i - 2))
    multiply(6)
    multiply(7)

    pga[dp] = (hg[...].astype(F32) * gelu_slope(acc[...])).astype(BF16)
    pgt = pga[dp]

    def rs_core(g):
        return send(tp.at[:, g, :, 1 - c], sr.at[:, g], rsc_s.at[g], rsc_r.at[g], sibling)

    def partial(i):
        g = group(ring(i))
        for y in range(NY):
            rows = pl.ds(pl.multiple_of((y * NG + g) * BLK, BLK), BLK)
            part = jnp.dot(wt[rows, :], pgt, preferred_element_type=F32)
            tp[y, g] = part.astype(BF16).reshape(NN, NC, CH, TOK)
        rs_core(g).start()

    def rs_near(g, e):
        dy, dz = near_off(e)
        src = pair.at[(yh + dy) % NY, g, (z + dz + NZ) % NN]
        return send(src, near_in.at[g, e - 1], rsn_s.at[g, e - 1], rsn_r.at[g, e - 1], at(dz, dy))

    def pair_up(i):
        g = group(ring(i))
        rs_core(g).wait_recv()
        for y in range(NY):
            pair[y, g] = (tp[y, g, :, c].astype(F32) + sr[y, g].astype(F32)).astype(BF16)
        for e in NEAR:
            rs_near(g, e).start()

    def near_sum(offset):
        g = group(offset)
        total = pair[yh, g, n].astype(F32)
        for e in NEAR:
            rs_near(g, e).wait_recv()
        for e in NEAR:
            total += near_in[g, e - 1].astype(F32)
        return total

    def rs_far(k):
        dz = (8, -8, 8 * sgn, 4, -4, 8 * sgn, -8 * sgn)[k]
        return send(far_out.at[k], far_in.at[k], rsf_s.at[k], rsf_r.at[k], at(dz))

    def rs_far_start(k, value):
        far_out[k] = value.astype(BF16)
        rs_far(k).start()

    def rs_far_got(k):
        rs_far(k).wait_recv()
        return far_in[k].astype(F32)

    def slice_of(p, half):
        return p // 4, 2 * (p % 4) + half

    def pg_send(r):
        return send(pga.at[dp], pga.at[dp], pg_s.at[r - 1], pg_r.at[r - 1], ((dp + r) % NDP, mp))

    def pg_got(r):
        ref = pga.at[(dp - r + NDP) % NDP]
        send(ref, ref, pg_s.at[r - 1], pg_r.at[r - 1], sibling).wait_recv()

    def xs_send(r):
        to = (dp + r) % NDP
        y, g = slice_of(to, c)
        return send(xt.at[y, g], xs.at[dp, c], xs_s.at[r - 1], xs_r.at[r - 1], (to, mp))

    def xs_got(r):
        ref = xs.at[(dp - r + NDP) % NDP, c]
        send(ref, ref, xs_s.at[r - 1], xs_r.at[r - 1], sibling).wait_recv()

    def xc_copy(r, half):
        ref = xs.at[(dp - r + NDP) % NDP, half]
        return send(ref, ref, xc_s.at[r - 1], xc_r.at[r - 1], sibling)

    loop(5, 8, partial)
    loop(3, 5, partial)
    loop(5, 8, pair_up)
    loop(1, 3, partial)
    loop(3, 5, pair_up)
    partial(0)
    loop(1, 3, pair_up)
    pair_up(0)
    for k in range(7):
        ag_far(k).wait_send()

    def ag_sent(g):
        for e in NEAR:
            ag_near(g, e).wait_send()
        ag_core(g, c).wait_send()

    loop(0, NG, ag_sent)

    rs_far_start(0, near_sum(3))
    rs_far_start(1, near_sum(-3))
    rs_far_start(2, near_sum(4))
    own_copies = []
    for half in range(2):
        y, g = slice_of(dp, half)
        own_copies.append(pltpu.make_async_copy(xt.at[y, g], xs.at[dp, half], own_sem.at[half]))
        own_copies[-1].start()
    for r in range(1, NDP):
        pg_send(r).start()
    for r in range(1, NDP):
        xs_send(r).start()
    rs_far_start(6, near_sum(-2 * sgn))
    ahead = near_sum(2 * sgn)
    right, left = near_sum(1), near_sum(-1)
    mine = near_sum(0)
    rs_far_start(5, ahead + rs_far_got(2))
    rs_far_start(3, right + rs_far_got(0))
    rs_far_start(4, left + rs_far_got(1))
    for r in range(1, NDP):
        xs_got(r)
        xc_copy(r, c).start()

    for copy in own_copies:
        copy.wait()
    for r in range(1, NDP):
        pg_got(r)
        xc_copy(r, 1 - c).wait_recv()

    def weight_rows(half):
        total = jnp.zeros((HID, BLK), F32)
        for p in range(NDP):
            total += lax.dot_general(
                pga[p], xs[p, half].reshape(BLK, TOK),
                (((1,), (1,)), ((), ())), preferred_element_type=F32,
            )
        wg[:, pl.ds(pl.multiple_of(half * BLK, BLK), BLK)] = total

    loop(0, 2, weight_rows)
    store_wg = pltpu.make_async_copy(wg, wg_hbm, out_sem.at[0])
    store_wg.start()

    def rs_sent(g):
        for e in NEAR:
            rs_near(g, e).wait_send()
        rs_core(g).wait_send()

    loop(0, NG, rs_sent)
    for r in range(1, NDP):
        pg_send(r).wait_send()
        xs_send(r).wait_send()
        xc_copy(r, c).wait_send()

    for k in (3, 4, 5, 6):
        mine += rs_far_got(k)
    tok[...] = mine.astype(BF16)
    store_tok = pltpu.make_async_copy(tok, tok_hbm, out_sem.at[1])
    store_tok.start()
    for k in range(7):
        rs_far(k).wait_send()
    store_wg.wait()
    store_tok.wait()


def local(tokens_in, in_weight, hidden_grad):
    vmem, dma = pltpu.VMEM, pltpu.SemaphoreType.DMA
    features = in_weight.shape[0]
    token_rows, weight_cols = pl.pallas_call(
        kernel,
        out_shape=(
            jax.ShapeDtypeStruct((CH, TOK), BF16),
            jax.ShapeDtypeStruct((HID, features // NDP), F32),
        ),
        in_specs=[pl.BlockSpec(memory_space=pl.ANY)] * 3,
        out_specs=(pl.BlockSpec(memory_space=pl.ANY),) * 2,
        scratch_shapes=[
            vmem((HID, features), BF16),
            vmem((features, HID), BF16),
            vmem((HID, TOK), BF16),
            vmem((CH, TOK), BF16),
            vmem((NY, NG, NN, NC, CH, TOK), BF16),
            vmem((HID, TOK), F32),
            vmem((NY, NG, NN, NC, CH, TOK), BF16),
            vmem((NY, NG, NN, CH, TOK), BF16),
            vmem((NY, NG, NN, CH, TOK), BF16),
            vmem((NG, 7, CH, TOK), BF16),
            vmem((7, CH, TOK), BF16),
            vmem((7, CH, TOK), BF16),
            vmem((NDP, 2, NN, NC, CH, TOK), BF16),
            vmem((NDP, HID, TOK), BF16),
            vmem((HID, features // NDP), F32),
            dma((3,)), dma((2,)), dma((2,)),
            dma((7,)), dma((7,)), dma((NG, 7)), dma((NG, 7)), dma((NG,)), dma((NG,)),
            dma((NG,)), dma((NG,)), dma((NG, 7)), dma((NG, 7)), dma((7,)), dma((7,)),
            dma((7,)), dma((7,)), dma((7,)), dma((7,)), dma((7,)), dma((7,)),
        ],
        compiler_params=pltpu.CompilerParams(
            collective_id=0, has_side_effects=True, vmem_limit_bytes=63 * 2**20
        ),
        cost_estimate=pl.CostEstimate(
            flops=6 * TOK * features * HID, bytes_accessed=4 * 2**20, transcendentals=2 * TOK * HID
        ),
    )(tokens_in.T, in_weight.T, hidden_grad.T)
    return token_rows.T, weight_cols.T


def solution(mesh):
    in_specs = (P("dp", "mp"), P(None, "mp"), P("dp", "mp"))
    out_specs = (P("dp", "mp"), P("dp", "mp"))
    return jax.shard_map(local, mesh=mesh, in_specs=in_specs, out_specs=out_specs, check_vma=False)
```

```python
import jax
import jax.numpy as jnp
from jax import lax
from jax.experimental import pallas as pl
from jax.experimental.pallas import tpu as pltpu
from jax.sharding import PartitionSpec as P

MESH = pl.DeviceIdType.MESH
F32, BF16 = jnp.float32, jnp.bfloat16

NY, NG, NN, NC, NZ, NDP = 2, 8, 4, 2, 32, 8
CH, TOK, HID = 48, 128, 192
BLK = NN * NC * CH
NEAR = range(1, 8)


def gelu_slope(value):
    normal_cdf = 0.5 * (1.0 + lax.erf(value * 0.7071067811865476))
    density = jnp.exp(-0.5 * value * value) * 0.3989422804014327
    return normal_cdf + value * density


def ring(i):
    return ((i + 1) // 2) * (2 * (i % 2) - 1)


def kernel(
    x_hbm, w_hbm, h_hbm, tok_hbm, wg_hbm,
    w, wt, hg, tok, xt, acc, tp, sr, pair, near_in, far_out, far_in, xs, pga, wg,
    in_sem, out_sem, own_sem,
    agf_s, agf_r, agn_s, agn_r, agc_s, agc_r,
    rsc_s, rsc_r, rsn_s, rsn_r, rsf_s, rsf_r,
    pg_s, pg_r, xs_s, xs_r, xc_s, xc_r,
):
    dp, mp = lax.axis_index("dp"), lax.axis_index("mp")
    yh, z, c = mp // 64, (mp // 2) % NZ, mp % 2
    g0, n = z // NN, z % NN
    sgn = 1 - 2 * c

    def at(dz, dy=0, core=c):
        return (dp, ((yh + dy) % NY) * 64 + ((z + dz + NZ) % NZ) * 2 + core)

    def send(src, dst, s, r, device):
        return pltpu.make_async_remote_copy(
            src_ref=src, dst_ref=dst, send_sem=s, recv_sem=r, device_id=device, device_id_type=MESH
        )

    def near_off(e):
        return e % 2, (0, 1, -1, 2 * sgn)[e // 2]

    def group(offset):
        return (g0 + offset + NG) % NG

    def target(r):
        return ((dp // 4 + r // 4) % 2) * 4 + (dp % 4 + r % 4) % 4

    def source(r):
        return ((dp // 4 + r // 4) % 2) * 4 + (dp % 4 - r % 4 + 4) % 4

    sibling = at(0, core=1 - c)
    far_z = (8, -8, 4, -4)

    load_x = pltpu.make_async_copy(x_hbm, xt.at[yh, g0, n, c], in_sem.at[0])
    load_w = pltpu.make_async_copy(w_hbm, w, in_sem.at[1])
    load_h = pltpu.make_async_copy(h_hbm, hg, in_sem.at[2])

    barrier = pltpu.get_barrier_semaphore()
    for dz in far_z:
        pl.semaphore_signal(barrier, inc=1, device_id=at(-dz), device_id_type=MESH)
    for e in NEAR:
        dy, dz = near_off(e)
        pl.semaphore_signal(barrier, inc=1, device_id=at(-dz, dy), device_id_type=MESH)
    pl.semaphore_signal(barrier, inc=1, device_id=sibling, device_id_type=MESH)
    for r in range(1, NDP):
        pl.semaphore_signal(barrier, inc=1, device_id=(source(r), mp), device_id_type=MESH)

    load_x.start()
    load_w.start()
    load_h.start()
    acc[...] = jnp.zeros_like(acc)
    load_x.wait()
    pl.semaphore_wait(barrier, 4 + 7 + 1 + 7)

    def ag_far(k):
        chunk = (0, 0, 0, 0, -2, 2, -2 * sgn)[k]
        dz = (8, -8, 4, -4, 4, -4, 8 * sgn)[k]
        ref = xt.at[yh, group(chunk), n, c]
        return send(ref, ref, agf_s.at[k], agf_r.at[k], at(dz))

    def ag_far_got(k):
        chunk = (-2, 2, -1, 1, -3, 3, 4)[k]
        ref = xt.at[yh, group(chunk), n, c]
        send(ref, ref, agf_s.at[k], agf_r.at[k], at(8)).wait_recv()

    def ag_near(g, e):
        dy, dz = near_off(e)
        ref = xt.at[yh, g, n, c]
        return send(ref, ref, agn_s.at[g, e - 1], agn_r.at[g, e - 1], at(dz, dy))

    def ag_near_start(i):
        g = group(ring(i))
        for e in NEAR:
            ag_near(g, e).start()

    def ag_near_got(g):
        for e in NEAR:
            dy, dz = near_off(e)
            ref = xt.at[(yh + dy) % NY, g, (z - dz + NZ) % NN, c]
            send(ref, ref, agn_s.at[g, e - 1], agn_r.at[g, e - 1], at(8)).wait_recv()

    def ag_core(g, core):
        ref = xt.at[:, g, :, core]
        return send(ref, ref, agc_s.at[g], agc_r.at[g], sibling)

    def weights_of(y, g):
        return w[:, pl.ds(pl.multiple_of((y * NG + g) * BLK, BLK), BLK)]

    def pass_on(i):
        g = group(ring(i))
        ag_near_got(g)
        ag_core(g, c).start()

    def multiply(i):
        g = group(ring(i))
        ag_core(g, 1 - c).wait_recv()
        total = acc[...]
        for y in range(NY):
            total += jnp.dot(
                weights_of(y, g), xt[y, g].reshape(BLK, TOK), preferred_element_type=F32
            )
        acc[...] = total

    def turn(b):
        at_b = pl.ds(pl.multiple_of(b * BLK, BLK), BLK)
        wt[at_b, :] = w[:, at_b].T

    def loop(low, high, *steps):
        def body(i, carry):
            for step in steps:
                step(i)
            return carry

        lax.fori_loop(low, high, body, 0)

    for k in range(4):
        ag_far(k).start()
    ag_near_start(0)
    load_w.wait()
    load_h.wait()
    loop(0, NY * NG, turn)
    ag_far_got(0)
    ag_far_got(1)
    for k in (6, 4, 5):
        ag_far(k).start()
    ag_far_got(2)
    ag_far_got(3)
    loop(1, 5, ag_near_start)
    pass_on(0)
    ag_far_got(4)
    ag_far_got(5)
    loop(5, 7, ag_near_start)
    ag_far_got(6)
    ag_near_start(7)
    pass_on(1)
    loop(2, 8, pass_on, lambda i: multiply(i - 2))
    multiply(6)
    multiply(7)

    pga[dp] = (hg[...].astype(F32) * gelu_slope(acc[...])).astype(BF16)
    pgt = pga[dp]

    def rs_core(g):
        return send(tp.at[:, g, :, 1 - c], sr.at[:, g], rsc_s.at[g], rsc_r.at[g], sibling)

    def partial(i):
        g = group(ring(i))
        for y in range(NY):
            rows = pl.ds(pl.multiple_of((y * NG + g) * BLK, BLK), BLK)
            part = jnp.dot(wt[rows, :], pgt, preferred_element_type=F32)
            tp[y, g] = part.astype(BF16).reshape(NN, NC, CH, TOK)
        rs_core(g).start()

    def rs_near(g, e):
        dy, dz = near_off(e)
        src = pair.at[(yh + dy) % NY, g, (z + dz + NZ) % NN]
        return send(src, near_in.at[g, e - 1], rsn_s.at[g, e - 1], rsn_r.at[g, e - 1], at(dz, dy))

    def pair_up(i):
        g = group(ring(i))
        rs_core(g).wait_recv()
        for y in range(NY):
            pair[y, g] = (tp[y, g, :, c].astype(F32) + sr[y, g].astype(F32)).astype(BF16)
        for e in NEAR:
            rs_near(g, e).start()

    def near_sum(offset):
        g = group(offset)
        total = pair[yh, g, n].astype(F32)
        for e in NEAR:
            rs_near(g, e).wait_recv()
        for e in NEAR:
            total += near_in[g, e - 1].astype(F32)
        return total

    def rs_far(k):
        dz = (8, -8, 8 * sgn, 4, -4, 8 * sgn, -8 * sgn)[k]
        return send(far_out.at[k], far_in.at[k], rsf_s.at[k], rsf_r.at[k], at(dz))

    def rs_far_start(k, value):
        far_out[k] = value.astype(BF16)
        rs_far(k).start()

    def rs_far_got(k):
        rs_far(k).wait_recv()
        return far_in[k].astype(F32)

    def slice_of(p, half):
        return p // 4, 2 * (p % 4) + half

    def pg_send(r):
        return send(pga.at[dp], pga.at[dp], pg_s.at[r - 1], pg_r.at[r - 1], (target(r), mp))

    def pg_got(r):
        ref = pga.at[source(r)]
        send(ref, ref, pg_s.at[r - 1], pg_r.at[r - 1], sibling).wait_recv()

    def xs_send(r):
        to = target(r)
        y, g = slice_of(to, c)
        return send(xt.at[y, g], xs.at[dp, c], xs_s.at[r - 1], xs_r.at[r - 1], (to, mp))

    def xs_got(r):
        ref = xs.at[source(r), c]
        send(ref, ref, xs_s.at[r - 1], xs_r.at[r - 1], sibling).wait_recv()

    def xc_copy(r, half):
        ref = xs.at[source(r), half]
        return send(ref, ref, xc_s.at[r - 1], xc_r.at[r - 1], sibling)

    def dp_send(low, high):
        for r in range(low, high):
            pg_send(r).start()
        for r in range(low, high):
            xs_send(r).start()

    def pass_halves(low, high):
        for r in range(low, high):
            xs_got(r)
            xc_copy(r, c).start()

    def weight_part(parts, first):
        def rows(half):
            cols = pl.ds(pl.multiple_of(half * BLK, BLK), BLK)
            total = jnp.zeros((HID, BLK), F32) if first else wg[:, cols]
            for r in parts:
                p = source(r)
                total += lax.dot_general(
                    pga[p], xs[p, half].reshape(BLK, TOK),
                    (((1,), (1,)), ((), ())), preferred_element_type=F32,
                )
            wg[:, cols] = total

        others = [r for r in parts if r]
        for r in others:
            pg_got(r)
        rows(c)
        for r in others:
            xc_copy(r, 1 - c).wait_recv()
        rows(1 - c)

    own_copies = []
    for half in range(2):
        y, g = slice_of(dp, half)
        own_copies.append(pltpu.make_async_copy(xt.at[y, g], xs.at[dp, half], own_sem.at[half]))
        own_copies[-1].start()
    loop(5, 8, partial)
    loop(3, 5, partial)
    loop(5, 8, pair_up)
    loop(1, 3, partial)
    loop(3, 5, pair_up)
    partial(0)
    loop(1, 3, pair_up)
    pair_up(0)
    dp_send(1, 4)
    for k in range(7):
        ag_far(k).wait_send()

    def ag_sent(g):
        for e in NEAR:
            ag_near(g, e).wait_send()
        ag_core(g, c).wait_send()

    loop(0, NG, ag_sent)

    rs_far_start(0, near_sum(3))
    rs_far_start(1, near_sum(-3))
    rs_far_start(2, near_sum(4))
    dp_send(4, 8)
    pass_halves(1, 4)
    rs_far_start(6, near_sum(-2 * sgn))
    ahead = near_sum(2 * sgn)
    right, left = near_sum(1), near_sum(-1)
    mine = near_sum(0)
    for copy in own_copies:
        copy.wait()
    weight_part((0, 1, 2, 3), True)

    rs_far_start(5, ahead + rs_far_got(2))
    rs_far_start(3, right + rs_far_got(0))
    rs_far_start(4, left + rs_far_got(1))

    def rs_sent(g):
        for e in NEAR:
            rs_near(g, e).wait_send()
        rs_core(g).wait_send()

    loop(0, NG, rs_sent)

    pass_halves(4, 8)
    weight_part((4, 5, 6, 7), False)
    store_wg = pltpu.make_async_copy(wg, wg_hbm, out_sem.at[0])
    store_wg.start()

    for r in range(1, NDP):
        pg_send(r).wait_send()
        xs_send(r).wait_send()
        xc_copy(r, c).wait_send()

    for k in (3, 4, 5, 6):
        mine += rs_far_got(k)
    tok[...] = mine.astype(BF16)
    store_tok = pltpu.make_async_copy(tok, tok_hbm, out_sem.at[1])
    store_tok.start()
    for k in range(7):
        rs_far(k).wait_send()
    store_wg.wait()
    store_tok.wait()


def store(tok_in, wg_in, tok_hbm, wg_hbm, sem):
    copies = [
        pltpu.make_async_copy(wg_in, wg_hbm, sem.at[0]),
        pltpu.make_async_copy(tok_in, tok_hbm, sem.at[1]),
    ]
    for copy in copies:
        copy.start()
    for copy in copies:
        copy.wait()


def local(tokens_in, in_weight, hidden_grad):
    vmem, dma = pltpu.VMEM, pltpu.SemaphoreType.DMA
    features = in_weight.shape[0]
    token_rows, weight_cols = pl.pallas_call(
        kernel,
        out_shape=(
            jax.ShapeDtypeStruct((CH, TOK), BF16),
            jax.ShapeDtypeStruct((HID, features // NDP), F32),
        ),
        in_specs=[pl.BlockSpec(memory_space=pl.ANY)] * 3,
        out_specs=(pl.BlockSpec(memory_space=pl.ANY),) * 2,
        scratch_shapes=[
            vmem((HID, features), BF16),
            vmem((features, HID), BF16),
            vmem((HID, TOK), BF16),
            vmem((CH, TOK), BF16),
            vmem((NY, NG, NN, NC, CH, TOK), BF16),
            vmem((HID, TOK), F32),
            vmem((NY, NG, NN, NC, CH, TOK), BF16),
            vmem((NY, NG, NN, CH, TOK), BF16),
            vmem((NY, NG, NN, CH, TOK), BF16),
            vmem((NG, 7, CH, TOK), BF16),
            vmem((7, CH, TOK), BF16),
            vmem((7, CH, TOK), BF16),
            vmem((NDP, 2, NN, NC, CH, TOK), BF16),
            vmem((NDP, HID, TOK), BF16),
            vmem((HID, features // NDP), F32),
            dma((3,)), dma((2,)), dma((2,)),
            dma((7,)), dma((7,)), dma((NG, 7)), dma((NG, 7)), dma((NG,)), dma((NG,)),
            dma((NG,)), dma((NG,)), dma((NG, 7)), dma((NG, 7)), dma((7,)), dma((7,)),
            dma((7,)), dma((7,)), dma((7,)), dma((7,)), dma((7,)), dma((7,)),
        ],
        compiler_params=pltpu.CompilerParams(
            collective_id=0, has_side_effects=True, vmem_limit_bytes=63 * 2**20
        ),
        cost_estimate=pl.CostEstimate(
            flops=6 * TOK * features * HID, bytes_accessed=4 * 2**20, transcendentals=2 * TOK * HID
        ),
    )(tokens_in.T, in_weight.T, hidden_grad.T)
    token_rows, weight_cols = pl.pallas_call(
        store,
        out_shape=(
            jax.ShapeDtypeStruct(token_rows.shape, BF16),
            jax.ShapeDtypeStruct(weight_cols.shape, F32),
        ),
        in_specs=[pl.BlockSpec(memory_space=pltpu.VMEM)] * 2,
        out_specs=(pl.BlockSpec(memory_space=pl.ANY),) * 2,
        scratch_shapes=[dma((2,))],
    )(token_rows, weight_cols)
    return token_rows.T, weight_cols.T


def solution(mesh):
    in_specs = (P("dp", "mp"), P(None, "mp"), P("dp", "mp"))
    out_specs = (P("dp", "mp"), P("dp", "mp"))
    return jax.shard_map(local, mesh=mesh, in_specs=in_specs, out_specs=out_specs, check_vma=False)
```

```python
import jax
import jax.numpy as jnp
from jax import lax
from jax.experimental import pallas as pl
from jax.experimental.pallas import tpu as pltpu
from jax.sharding import PartitionSpec as P

MESH = pl.DeviceIdType.MESH
F32, BF16 = jnp.float32, jnp.bfloat16

NY, NG, NN, NC, NZ, NDP = 2, 8, 4, 2, 32, 8
CH, TOK, HID = 48, 128, 192
BLK = NN * NC * CH
NEAR = range(1, 8)


def gelu_slope(value):
    normal_cdf = 0.5 * (1.0 + lax.erf(value * 0.7071067811865476))
    density = jnp.exp(-0.5 * value * value) * 0.3989422804014327
    return normal_cdf + value * density


def ring(i):
    return ((i + 1) // 2) * (2 * (i % 2) - 1)


def kernel(
    x_hbm, w_hbm, h_hbm, tok_hbm, wg_hbm,
    w, wt, hg, tok, xt, acc, tp, sr, pair, near_in, far_out, far_in, xs, pga, wg,
    in_sem, out_sem, own_sem,
    agf_s, agf_r, agn_s, agn_r, agc_s, agc_r,
    rsc_s, rsc_r, rsn_s, rsn_r, rsf_s, rsf_r,
    pg_s, pg_r, xs_s, xs_r, xc_s, xc_r,
):
    dp, mp = lax.axis_index("dp"), lax.axis_index("mp")
    yh, z, c = mp // 64, (mp // 2) % NZ, mp % 2
    g0, n = z // NN, z % NN
    sgn = 1 - 2 * c

    def at(dz, dy=0, core=c):
        return (dp, ((yh + dy) % NY) * 64 + ((z + dz + NZ) % NZ) * 2 + core)

    def send(src, dst, s, r, device):
        return pltpu.make_async_remote_copy(
            src_ref=src, dst_ref=dst, send_sem=s, recv_sem=r, device_id=device, device_id_type=MESH
        )

    def near_off(e):
        return e % 2, (0, 1, -1, 2 * sgn)[e // 2]

    def group(offset):
        return (g0 + offset + NG) % NG

    def target(r):
        return ((dp // 4 + r // 4) % 2) * 4 + (dp % 4 + r % 4) % 4

    def source(r):
        return ((dp // 4 + r // 4) % 2) * 4 + (dp % 4 - r % 4 + 4) % 4

    sibling = at(0, core=1 - c)
    far_z = (8, -8, 4, -4)

    load_x = pltpu.make_async_copy(x_hbm, xt.at[yh, g0, n, c], in_sem.at[0])
    load_w = pltpu.make_async_copy(w_hbm, w, in_sem.at[1])
    load_h = pltpu.make_async_copy(h_hbm, hg, in_sem.at[2])

    barrier = pltpu.get_barrier_semaphore()
    for dz in far_z:
        pl.semaphore_signal(barrier, inc=1, device_id=at(-dz), device_id_type=MESH)
    for e in NEAR:
        dy, dz = near_off(e)
        pl.semaphore_signal(barrier, inc=1, device_id=at(-dz, dy), device_id_type=MESH)
    pl.semaphore_signal(barrier, inc=1, device_id=sibling, device_id_type=MESH)
    for r in range(1, NDP):
        pl.semaphore_signal(barrier, inc=1, device_id=(source(r), mp), device_id_type=MESH)

    load_x.start()
    load_w.start()
    load_h.start()
    acc[...] = jnp.zeros_like(acc)
    load_x.wait()
    pl.semaphore_wait(barrier, 4 + 7 + 1 + 7)

    def ag_far(k):
        chunk = (0, 0, 0, 0, -2, 2, -2 * sgn)[k]
        dz = (8, -8, 4, -4, 4, -4, 8 * sgn)[k]
        ref = xt.at[yh, group(chunk), n, c]
        return send(ref, ref, agf_s.at[k], agf_r.at[k], at(dz))

    def ag_far_got(k):
        chunk = (-2, 2, -1, 1, -3, 3, 4)[k]
        ref = xt.at[yh, group(chunk), n, c]
        send(ref, ref, agf_s.at[k], agf_r.at[k], at(8)).wait_recv()

    def ag_near(g, e):
        dy, dz = near_off(e)
        ref = xt.at[yh, g, n, c]
        return send(ref, ref, agn_s.at[g, e - 1], agn_r.at[g, e - 1], at(dz, dy))

    def ag_near_start(i):
        g = group(ring(i))
        for e in NEAR:
            ag_near(g, e).start()

    def ag_near_got(g):
        for e in NEAR:
            dy, dz = near_off(e)
            ref = xt.at[(yh + dy) % NY, g, (z - dz + NZ) % NN, c]
            send(ref, ref, agn_s.at[g, e - 1], agn_r.at[g, e - 1], at(8)).wait_recv()

    def ag_core(g, core):
        ref = xt.at[:, g, :, core]
        return send(ref, ref, agc_s.at[g], agc_r.at[g], sibling)

    def weights_of(y, g):
        return w[:, pl.ds(pl.multiple_of((y * NG + g) * BLK, BLK), BLK)]

    def pass_on(i):
        g = group(ring(i))
        ag_near_got(g)
        ag_core(g, c).start()

    def multiply(i):
        g = group(ring(i))
        ag_core(g, 1 - c).wait_recv()
        total = acc[...]
        for y in range(NY):
            total += jnp.dot(
                weights_of(y, g), xt[y, g].reshape(BLK, TOK), preferred_element_type=F32
            )
        acc[...] = total

    def turn(b):
        at_b = pl.ds(pl.multiple_of(b * BLK, BLK), BLK)
        wt[at_b, :] = w[:, at_b].T

    def loop(low, high, *steps):
        def body(i, carry):
            for step in steps:
                step(i)
            return carry

        lax.fori_loop(low, high, body, 0)

    for k in range(4):
        ag_far(k).start()
    ag_near_start(0)
    load_w.wait()
    load_h.wait()
    loop(0, NY * NG, turn)
    ag_far_got(0)
    ag_far_got(1)
    for k in (6, 4, 5):
        ag_far(k).start()
    ag_far_got(2)
    ag_far_got(3)
    loop(1, 5, ag_near_start)
    pass_on(0)
    ag_far_got(4)
    ag_far_got(5)
    loop(5, 7, ag_near_start)
    ag_far_got(6)
    ag_near_start(7)
    pass_on(1)
    loop(2, 8, pass_on, lambda i: multiply(i - 2))
    multiply(6)
    multiply(7)

    pga[dp] = (hg[...].astype(F32) * gelu_slope(acc[...])).astype(BF16)
    pgt = pga[dp]

    def rs_core(g):
        return send(tp.at[:, g, :, 1 - c], sr.at[:, g], rsc_s.at[g], rsc_r.at[g], sibling)

    def partial(i):
        g = group(ring(i))
        for y in range(NY):
            rows = pl.ds(pl.multiple_of((y * NG + g) * BLK, BLK), BLK)
            part = jnp.dot(wt[rows, :], pgt, preferred_element_type=F32)
            tp[y, g] = part.astype(BF16).reshape(NN, NC, CH, TOK)
        rs_core(g).start()

    def rs_near(g, e):
        dy, dz = near_off(e)
        src = pair.at[(yh + dy) % NY, g, (z + dz + NZ) % NN]
        return send(src, near_in.at[g, e - 1], rsn_s.at[g, e - 1], rsn_r.at[g, e - 1], at(dz, dy))

    def pair_up(i):
        g = group(ring(i))
        rs_core(g).wait_recv()
        for y in range(NY):
            pair[y, g] = (tp[y, g, :, c].astype(F32) + sr[y, g].astype(F32)).astype(BF16)
        for e in NEAR:
            rs_near(g, e).start()

    def near_sum(offset):
        g = group(offset)
        total = pair[yh, g, n].astype(F32)
        for e in NEAR:
            rs_near(g, e).wait_recv()
        for e in NEAR:
            total += near_in[g, e - 1].astype(F32)
        return total

    def rs_far(k):
        dz = (8, -8, 8 * sgn, 4, -4, 8 * sgn, -8 * sgn)[k]
        return send(far_out.at[k], far_in.at[k], rsf_s.at[k], rsf_r.at[k], at(dz))

    def rs_far_start(k, value):
        far_out[k] = value.astype(BF16)
        rs_far(k).start()

    def rs_far_got(k):
        rs_far(k).wait_recv()
        return far_in[k].astype(F32)

    def slice_of(p, half):
        return p // 4, 2 * (p % 4) + half

    def pg_send(r):
        return send(pga.at[dp], pga.at[dp], pg_s.at[r - 1], pg_r.at[r - 1], (target(r), mp))

    def pg_got(r):
        ref = pga.at[source(r)]
        send(ref, ref, pg_s.at[r - 1], pg_r.at[r - 1], sibling).wait_recv()

    def xs_send(r):
        to = target(r)
        y, g = slice_of(to, c)
        return send(xt.at[y, g], xs.at[dp, c], xs_s.at[r - 1], xs_r.at[r - 1], (to, mp))

    def xs_got(r):
        ref = xs.at[source(r), c]
        send(ref, ref, xs_s.at[r - 1], xs_r.at[r - 1], sibling).wait_recv()

    def xc_copy(r, half):
        ref = xs.at[source(r), half]
        return send(ref, ref, xc_s.at[r - 1], xc_r.at[r - 1], sibling)

    def dp_send(low, high):
        for r in range(low, high):
            xs_send(r).start()
        for r in range(low, high):
            pg_send(r).start()

    def pass_halves(low, high):
        for r in range(low, high):
            xs_got(r)
            xc_copy(r, c).start()

    def weight_part(parts, first):
        def rows(half):
            cols = pl.ds(pl.multiple_of(half * BLK, BLK), BLK)
            total = jnp.zeros((HID, BLK), F32) if first else wg[:, cols]
            for r in parts:
                p = source(r)
                total += lax.dot_general(
                    pga[p], xs[p, half].reshape(BLK, TOK),
                    (((1,), (1,)), ((), ())), preferred_element_type=F32,
                )
            wg[:, cols] = total

        others = [r for r in parts if r]
        for r in others:
            pg_got(r)
        rows(c)
        for r in others:
            xc_copy(r, 1 - c).wait_recv()
        rows(1 - c)

    own_copies = []
    for half in range(2):
        y, g = slice_of(dp, half)
        own_copies.append(pltpu.make_async_copy(xt.at[y, g], xs.at[dp, half], own_sem.at[half]))
        own_copies[-1].start()
    loop(5, 8, partial)
    loop(3, 5, partial)
    loop(5, 8, pair_up)
    loop(1, 3, partial)
    loop(3, 5, pair_up)
    partial(0)
    loop(1, 3, pair_up)
    pair_up(0)
    dp_send(1, 4)
    for k in range(7):
        ag_far(k).wait_send()

    def ag_sent(g):
        for e in NEAR:
            ag_near(g, e).wait_send()
        ag_core(g, c).wait_send()

    loop(0, NG, ag_sent)

    rs_far_start(0, near_sum(3))
    rs_far_start(1, near_sum(-3))
    rs_far_start(2, near_sum(4))
    dp_send(4, 8)
    pass_halves(1, 4)
    rs_far_start(6, near_sum(-2 * sgn))
    ahead = near_sum(2 * sgn)
    right, left = near_sum(1), near_sum(-1)
    mine = near_sum(0)
    for copy in own_copies:
        copy.wait()
    weight_part((0, 1, 2, 3), True)

    rs_far_start(5, ahead + rs_far_got(2))
    rs_far_start(3, right + rs_far_got(0))
    rs_far_start(4, left + rs_far_got(1))

    def rs_sent(g):
        for e in NEAR:
            rs_near(g, e).wait_send()
        rs_core(g).wait_send()

    loop(0, NG, rs_sent)

    pass_halves(4, 8)
    weight_part((4, 5, 6, 7), False)
    store_wg = pltpu.make_async_copy(wg, wg_hbm, out_sem.at[0])
    store_wg.start()

    for r in range(1, NDP):
        pg_send(r).wait_send()
        xs_send(r).wait_send()
        xc_copy(r, c).wait_send()

    for k in (3, 4, 5, 6):
        mine += rs_far_got(k)
    tok[...] = mine.astype(BF16)
    store_tok = pltpu.make_async_copy(tok, tok_hbm, out_sem.at[1])
    store_tok.start()
    for k in range(7):
        rs_far(k).wait_send()
    store_wg.wait()
    store_tok.wait()


def store(tok_in, wg_in, tok_hbm, wg_hbm, sem):
    copies = [
        pltpu.make_async_copy(wg_in, wg_hbm, sem.at[0]),
        pltpu.make_async_copy(tok_in, tok_hbm, sem.at[1]),
    ]
    for copy in copies:
        copy.start()
    for copy in copies:
        copy.wait()


def local(tokens_in, in_weight, hidden_grad):
    vmem, dma = pltpu.VMEM, pltpu.SemaphoreType.DMA
    features = in_weight.shape[0]
    token_rows, weight_cols = pl.pallas_call(
        kernel,
        out_shape=(
            jax.ShapeDtypeStruct((CH, TOK), BF16),
            jax.ShapeDtypeStruct((HID, features // NDP), F32),
        ),
        in_specs=[pl.BlockSpec(memory_space=pl.ANY)] * 3,
        out_specs=(pl.BlockSpec(memory_space=pl.ANY),) * 2,
        scratch_shapes=[
            vmem((HID, features), BF16),
            vmem((features, HID), BF16),
            vmem((HID, TOK), BF16),
            vmem((CH, TOK), BF16),
            vmem((NY, NG, NN, NC, CH, TOK), BF16),
            vmem((HID, TOK), F32),
            vmem((NY, NG, NN, NC, CH, TOK), BF16),
            vmem((NY, NG, NN, CH, TOK), BF16),
            vmem((NY, NG, NN, CH, TOK), BF16),
            vmem((NG, 7, CH, TOK), BF16),
            vmem((7, CH, TOK), BF16),
            vmem((7, CH, TOK), BF16),
            vmem((NDP, 2, NN, NC, CH, TOK), BF16),
            vmem((NDP, HID, TOK), BF16),
            vmem((HID, features // NDP), F32),
            dma((3,)), dma((2,)), dma((2,)),
            dma((7,)), dma((7,)), dma((NG, 7)), dma((NG, 7)), dma((NG,)), dma((NG,)),
            dma((NG,)), dma((NG,)), dma((NG, 7)), dma((NG, 7)), dma((7,)), dma((7,)),
            dma((7,)), dma((7,)), dma((7,)), dma((7,)), dma((7,)), dma((7,)),
        ],
        compiler_params=pltpu.CompilerParams(
            collective_id=0, has_side_effects=True, vmem_limit_bytes=63 * 2**20
        ),
        cost_estimate=pl.CostEstimate(
            flops=6 * TOK * features * HID, bytes_accessed=4 * 2**20, transcendentals=2 * TOK * HID
        ),
    )(tokens_in.T, in_weight.T, hidden_grad.T)
    token_rows, weight_cols = pl.pallas_call(
        store,
        out_shape=(
            jax.ShapeDtypeStruct(token_rows.shape, BF16),
            jax.ShapeDtypeStruct(weight_cols.shape, F32),
        ),
        in_specs=[pl.BlockSpec(memory_space=pltpu.VMEM)] * 2,
        out_specs=(pl.BlockSpec(memory_space=pl.ANY),) * 2,
        scratch_shapes=[dma((2,))],
    )(token_rows, weight_cols)
    return token_rows.T, weight_cols.T


def solution(mesh):
    in_specs = (P("dp", "mp"), P(None, "mp"), P("dp", "mp"))
    out_specs = (P("dp", "mp"), P("dp", "mp"))
    return jax.shard_map(local, mesh=mesh, in_specs=in_specs, out_specs=out_specs, check_vma=False)
```
